32 devices in a mesh: dp: 8 (over y, x, core), seq: 4 (over z).
Axes of the slice: x: 2, y: 2, z: 4, core: 2. Of those that a mesh axis runs over, the one named last changes fastest.
Arguments:
- pre_activation: bfloat16 [8, 16, 128, 512], P('dp', None, 'seq'), may hold values from -6 to 6
- output_grad: bfloat16 [8, 16, 128, 512], P('dp', None, 'seq'), may hold values from -0.59765625 to 0.59765625
- up_kernel: bfloat16 [3, 3, 512, 512], replicated, may hold values from -0.09375 to 0.09375
- in_kernel: bfloat16 [3, 3, 16, 512], replicated, may hold values from -0.09375 to 0.09375
- final_weight: bfloat16 [64, 3072], replicated, may hold values from -0.75 to 0.75
- gate_table: bfloat16 [8, 3072], replicated, may hold values from -4 to 4
- bucket: int32 [8], P('dp'), may hold values from 0 to 7
- query_vectors: bfloat16 [8, 512, 2048], P('dp', 'seq'), may hold values from -12 to 12
- key_vectors: bfloat16 [8, 512, 2048], P('dp', 'seq'), may hold values from -12 to 12
- value_vectors: bfloat16 [8, 512, 2048], P('dp', 'seq'), may hold values from -6 to 6
- out_weight: bfloat16 [2048, 3072], replicated, may hold values from -1.796875 to 1.796875
- block_input: bfloat16 [8, 512, 3072], P('dp', 'seq'), may hold values from -6 to 6
Outputs:
- query_grad: bfloat16 [8, 512, 2048], P('dp', 'seq')
- key_grad: bfloat16 [8, 512, 2048], P('dp', 'seq')
- value_grad: bfloat16 [8, 512, 2048], P('dp', 'seq')
- weight_grad: float32 [3072, 2048], P(('dp', 'seq'))
The draws below stay inside these ranges and needn't reach their ends.
All inputs are finite; a program needn't handle non-finite values.
Results may differ from the reference program's by a relative error of at most 0.025.
Values may be sent and summed in bfloat16 or wider, within the bound.
A program may use at most 192 MiB of HBM per device.

```python
import jax
import jax.numpy as jnp
from jax import lax

D = 3072
DH = 128
CH = 512
LAT_CH = 16
HEADS = 16
PW = 64
NB = 8
TOK_DEV = 128
IMG = 8
L = 512
PH = 8
LAT_H = 16
LAT_W = 128
ATT = 2048
N_SEQ = 4


def attention_pair(key):
    base = jax.random.fold_in(key, 7177)
    streams = jax.random.split(base, 2)
    shape = (IMG, L, HEADS * DH)
    queries = 1.5 * jnp.clip(jax.random.normal(streams[0], shape, jnp.float32), -4.0, 4.0)
    key_rows = 1.5 * jnp.clip(jax.random.normal(streams[1], shape, jnp.float32), -4.0, 4.0)
    return (queries, key_rows)


def draw_query_vectors(key, part):
    return attention_pair(key)[0].astype(jnp.bfloat16)


def draw_key_vectors(key, part):
    return attention_pair(key)[1].astype(jnp.bfloat16)


def touch_ends(drawn, rng, least, high):
    longest = drawn.shape.index(max(drawn.shape))
    spots = []
    for shift in (0, 1):
        where = [jax.random.randint(jax.random.fold_in(rng, axis), (), 0, length) for axis, length in enumerate(drawn.shape)]
        where[longest] = (where[longest] + shift) % drawn.shape[longest]
        spots.append(tuple(where))
    return drawn.at[spots[0]].set(least).at[spots[1]].set(high)


def steps_of(rng, extent, pieces, smallest, largest):
    factor_of, own = 1.0, jax.random.fold_in(rng, 6)
    for axis_at, parts in pieces:
        steps = jnp.exp(jax.random.uniform(jax.random.fold_in(own, axis_at), (parts,), jnp.float32, smallest / len(pieces), largest / len(pieces)))
        factor_of = factor_of * jnp.repeat(steps, extent[axis_at] // parts).reshape([-1 if axis == axis_at else 1 for axis in range(len(extent))])
    return factor_of


def scatter_about(own_key, extent, width, reach, pieces=(), kind=jnp.bfloat16):
    result = jax.random.normal(own_key, extent, jnp.float32) * width
    if len(pieces) > 0:
        result = steps_of(own_key, extent, pieces, -0.22, 0.18) * result
    return jnp.clip(result, min=-reach, max=reach).astype(kind)


def setup_inputs(seed: int = 0) -> dict:
    streams_of = jax.random.split(jax.random.key(seed), 13)
    pre_activation = scatter_about(streams_of[0], (IMG, LAT_H, LAT_W, CH), 1.0, 6.0, ((0, 8), (2, 4)))
    output_grad = scatter_about(streams_of[1], (IMG, LAT_H, LAT_W, CH), 0.1, 0.59765625, ((0, 8), (2, 4)))
    up_kernel = scatter_about(streams_of[2], (3, 3, CH, CH), (9 * CH) ** -0.5, 0.09375)
    in_kernel = scatter_about(streams_of[3], (3, 3, LAT_CH, CH), (9 * CH) ** -0.5, 0.09375)
    final_weight = scatter_about(streams_of[4], (4 * LAT_CH, D), (4 * LAT_CH) ** -0.5, 0.75)
    gate_table = scatter_about(streams_of[5], (NB, D), 1.0, 4.0)
    bucket = touch_ends(jax.random.randint(streams_of[6], (IMG,), 0, NB), jax.random.fold_in(streams_of[6], 1), 0, NB - 1).astype(jnp.int32)
    query_vectors = draw_query_vectors(jax.random.fold_in(streams_of[12], 71), 0)
    key_vectors = draw_key_vectors(jax.random.fold_in(streams_of[12], 71), 0)
    value_vectors = scatter_about(streams_of[9], (IMG, L, ATT), 1.0, 6.0, ((0, 8), (1, 4)))
    out_weight = scatter_about(streams_of[10], (ATT, D), 0.3, 1.796875)
    block_input = scatter_about(streams_of[11], (IMG, L, D), 1.0, 6.0, ((0, 8), (1, 4)))
    return dict(pre_activation=pre_activation, output_grad=output_grad, up_kernel=up_kernel, in_kernel=in_kernel, final_weight=final_weight, gate_table=gate_table, bucket=bucket, query_vectors=query_vectors, key_vectors=key_vectors, value_vectors=value_vectors, out_weight=out_weight, block_input=block_input)


def silu_slope(values):
    sigma = jax.nn.sigmoid(values)
    return sigma * (1.0 + values * (1.0 - sigma))


def transpose_conv(grad, kernel):
    flipped = jnp.transpose(kernel[::-1, ::-1], (0, 1, 3, 2))
    return lax.conv_general_dilated(grad, flipped, (1, 1), ((1, 1), (1, 1)), dimension_numbers=("NHWC", "HWIO", "NHWC"), preferred_element_type=jnp.float32)


def join_heads(stacked):
    return jnp.transpose(stacked, (1, 0, 2)).reshape(stacked.shape[1], stacked.shape[0] * stacked.shape[2])


def reference(pre_activation, output_grad, up_kernel, in_kernel, final_weight, gate_table, bucket, query_vectors, key_vectors, value_vectors, out_weight, block_input):
    softmax_scale = DH ** -0.5

    def one_image(total, inputs):
        feature_pre, cot_image, bucket_id, queries, key_rows, value_rows, input_rows = inputs
        act_grad = transpose_conv(cot_image[None], up_kernel)[0]
        feat_grad = (act_grad * silu_slope(feature_pre.astype(jnp.float32))).astype(jnp.bfloat16)
        latent_grad = transpose_conv(feat_grad[None], in_kernel)[0].astype(jnp.bfloat16)
        patches = latent_grad.reshape(PH, 2, PW, 2, LAT_CH).transpose(0, 2, 1, 3, 4).reshape(L, 4 * LAT_CH)
        stream_grad = jnp.dot(patches, final_weight, preferred_element_type=jnp.float32)
        picker = (jnp.arange(NB, dtype=jnp.int32) == bucket_id).astype(jnp.float32)
        gate_row = jnp.dot(picker, gate_table.astype(jnp.float32), precision=lax.Precision.HIGHEST)
        branch_grad = (stream_grad * gate_row[None, :]).astype(jnp.bfloat16)
        attn_grad = lax.dot_general(branch_grad, out_weight, (((1,), (1,)), ((), ())), preferred_element_type=jnp.float32).astype(jnp.bfloat16)

        def one_head(head):
            start = head * DH
            q_head = lax.dynamic_slice_in_dim(queries, start, DH, 1)
            k_head = lax.dynamic_slice_in_dim(key_rows, start, DH, 1)
            v_head = lax.dynamic_slice_in_dim(value_rows, start, DH, 1)
            g_head = lax.dynamic_slice_in_dim(attn_grad, start, DH, 1)
            scores = lax.dot_general(q_head, k_head, (((1,), (1,)), ((), ())), preferred_element_type=jnp.float32) * softmax_scale
            top = jnp.max(scores, axis=1, keepdims=True)
            weights = jnp.exp(scores - top)
            probs = weights / jnp.sum(weights, axis=1, keepdims=True)
            probs_low = probs.astype(jnp.bfloat16)
            head_out = jnp.dot(probs_low, v_head, preferred_element_type=jnp.float32).astype(jnp.bfloat16)
            row_dot = jnp.sum(g_head.astype(jnp.float32) * head_out.astype(jnp.float32), axis=1, keepdims=True)
            prob_grad = lax.dot_general(g_head, v_head, (((1,), (1,)), ((), ())), preferred_element_type=jnp.float32)
            score_grad = (probs * (prob_grad - row_dot)).astype(jnp.bfloat16)
            q_grad = (jnp.dot(score_grad, k_head, preferred_element_type=jnp.float32) * softmax_scale).astype(jnp.bfloat16)
            logit_tiles = score_grad.reshape(N_SEQ, TOK_DEV, L).astype(jnp.float32)
            query_tiles = q_head.reshape(N_SEQ, TOK_DEV, DH).astype(jnp.float32)
            key_portion = (jnp.einsum("jnp,jnt->jpt", logit_tiles, query_tiles) * softmax_scale).astype(jnp.bfloat16)
            probability_tiles = probs_low.reshape(N_SEQ, TOK_DEV, L).astype(jnp.float32)
            gradient_tiles = g_head.reshape(N_SEQ, TOK_DEV, DH).astype(jnp.float32)
            value_portion = jnp.einsum("jnp,jnt->jpt", probability_tiles, gradient_tiles).astype(jnp.bfloat16)
            k_grad = jnp.sum(key_portion.astype(jnp.float32), axis=0).astype(jnp.bfloat16)
            v_grad = jnp.sum(value_portion.astype(jnp.float32), axis=0).astype(jnp.bfloat16)
            return q_grad, k_grad, v_grad

        q_all, k_all, v_all = lax.map(one_head, jnp.arange(HEADS, dtype=jnp.int32))
        value_joined = join_heads(v_all)
        term = lax.dot_general(input_rows, value_joined, (((0,), (0,)), ((), ())), preferred_element_type=jnp.float32)
        return total + term, (join_heads(q_all), join_heads(k_all), value_joined)

    start_total = jnp.zeros((D, ATT), jnp.float32)
    weight_grad, grads = lax.scan(one_image, start_total, (pre_activation, output_grad, bucket, query_vectors, key_vectors, value_vectors, block_input))
    return grads[0], grads[1], grads[2], weight_grad
```

```python
import jax
import jax.numpy as jnp
from jax import lax
from jax.experimental import pallas as pl
from jax.experimental.pallas import tpu as pltpu
from jax.sharding import PartitionSpec as P

DH = 128


def silu_slope(values):
    sigma = jax.nn.sigmoid(values)
    return sigma * (1.0 + values * (1.0 - sigma))


def conv_grad(grad, kernel, rows_pad):
    flipped = jnp.transpose(kernel[::-1, ::-1], (0, 1, 3, 2))
    return lax.conv_general_dilated(
        grad,
        flipped,
        (1, 1),
        (rows_pad, (0, 0)),
        dimension_numbers=("NHWC", "HWIO", "NHWC"),
        preferred_element_type=jnp.float32,
    )


def head_kernel(q_ref, k_ref, v_ref, g_ref, qk_out, v_out):
    softmax_scale = DH ** (-0.5)
    blocks, _, rows, _ = q_ref.shape
    full = blocks * rows
    q_head = q_ref[:, 0].reshape(full, DH)
    k_head = k_ref[:, 0].reshape(full, DH)
    v_head = v_ref[:, 0].reshape(full, DH)
    g_head = g_ref[...]

    def rows_by_rows(a, b):
        return lax.dot_general(a, b, (((1,), (1,)), ((), ())), preferred_element_type=jnp.float32)

    def columns_by_columns(a, b):
        return lax.dot_general(a, b, (((0,), (0,)), ((), ())), preferred_element_type=jnp.float32)

    scores = rows_by_rows(q_head, k_head) * softmax_scale
    weights = jnp.exp(scores - jnp.max(scores, axis=1, keepdims=True))
    probs = weights * (1.0 / jnp.sum(weights, axis=1, keepdims=True))
    probs_low = probs.astype(jnp.bfloat16)
    head_out = jnp.dot(probs_low, v_head, preferred_element_type=jnp.float32).astype(jnp.bfloat16)
    row_dot = jnp.sum(
        g_head.astype(jnp.float32) * head_out.astype(jnp.float32), axis=1, keepdims=True
    )
    prob_grad = rows_by_rows(g_head, v_head)
    score_grad = (probs * (prob_grad - row_dot)).astype(jnp.bfloat16)
    q_grad = jnp.dot(score_grad, k_head, preferred_element_type=jnp.float32) * softmax_scale
    k_grad = columns_by_columns(score_grad, q_head) * softmax_scale
    v_grad = columns_by_columns(probs_low, g_head)
    qk_out[:, 0] = q_grad.astype(jnp.bfloat16).reshape(blocks, rows, DH)
    qk_out[:, 1] = k_grad.astype(jnp.bfloat16).reshape(blocks, rows, DH)
    v_out[...] = v_grad.astype(jnp.bfloat16).reshape(blocks, rows, DH)


def attention_backward(qkv, grad):
    blocks, _, rows, group = qkv.shape
    full = blocks * rows

    def part(which):
        return pl.BlockSpec((blocks, 1, rows, DH), lambda h: (0, which, 0, h))

    heads = group // DH
    return pl.pallas_call(
        head_kernel,
        grid=(heads,),
        in_specs=[part(0), part(1), part(2), pl.BlockSpec((full, DH), lambda h: (0, h))],
        out_specs=[
            pl.BlockSpec((blocks, 2, rows, DH), lambda h: (0, 0, 0, h)),
            pl.BlockSpec((blocks, rows, DH), lambda h: (0, 0, h)),
        ],
        out_shape=[
            jax.ShapeDtypeStruct((blocks, 2, rows, group), jnp.bfloat16),
            jax.ShapeDtypeStruct((blocks, rows, group), jnp.bfloat16),
        ],
        compiler_params=pltpu.CompilerParams(vmem_limit_bytes=48 * 2**20),
        cost_estimate=pl.CostEstimate(
            flops=14 * heads * full * full * DH,
            bytes_accessed=14 * full * group,
            transcendentals=heads * full * full,
        ),
    )(qkv, qkv, qkv, grad)


def per_device(
    pre_activation,
    output_grad,
    up_kernel,
    in_kernel,
    final_weight,
    gate_table,
    bucket,
    query_vectors,
    key_vectors,
    value_vectors,
    out_weight,
    block_input,
):
    seq_count = lax.axis_size("seq")
    dp_count = lax.axis_size("dp")
    seq_index = lax.axis_index("seq")
    tokens, width = query_vectors.shape[1:]
    group = width // seq_count
    full = tokens * seq_count
    model = block_input.shape[2]

    forward = [(i, i + 1) for i in range(seq_count - 1)]
    backward = [(target, source) for source, target in forward]
    low = lax.ppermute(
        jnp.concatenate([output_grad[:, :, -2:], pre_activation[:, :, -1:]], axis=2), "seq", forward
    )
    high = lax.ppermute(
        jnp.concatenate([output_grad[:, :, :2], pre_activation[:, :, :1]], axis=2), "seq", backward
    )
    qkv = jnp.stack([query_vectors[0], key_vectors[0], value_vectors[0]])
    qkv = qkv.reshape(3, tokens, seq_count, group).transpose(2, 0, 1, 3)
    qkv = lax.all_to_all(qkv, "seq", split_axis=0, concat_axis=0, tiled=True)
    rows_block = model // dp_count
    inputs = block_input[0].reshape(tokens, dp_count, rows_block).transpose(1, 0, 2)
    inputs = lax.all_to_all(inputs, "dp", split_axis=0, concat_axis=0, tiled=True)
    inputs = inputs.reshape(dp_count * tokens, rows_block)

    wide_grad = jnp.concatenate([low[:, :, :2], output_grad, high[:, :, :2]], axis=2)
    wide_pre = jnp.concatenate([low[:, :, 2:], pre_activation, high[:, :, 2:]], axis=2)
    act_grad = conv_grad(wide_grad, up_kernel, (1, 1))
    columns = jnp.arange(wide_pre.shape[2])
    inside = ((columns > 0) | (seq_index > 0)) & (
        (columns < wide_pre.shape[2] - 1) | (seq_index < seq_count - 1)
    )
    feat_grad = act_grad * silu_slope(wide_pre.astype(jnp.float32))
    feat_grad = jnp.where(inside[None, None, :, None], feat_grad, 0.0).astype(jnp.bfloat16)
    latent_grad = conv_grad(feat_grad, in_kernel, (1, 1)).astype(jnp.bfloat16)

    _, lat_rows, lat_cols, channels = latent_grad.shape
    patch_rows, patch_cols = lat_rows // 2, lat_cols // 2
    patches = (
        latent_grad.reshape(patch_rows, 2, patch_cols, 2, channels)
        .transpose(0, 2, 1, 3, 4)
        .reshape(1, patch_rows * patch_cols, 4 * channels)
    )
    patches = jnp.broadcast_to(patches, (seq_count,) + patches.shape[1:])
    patches = lax.all_to_all(patches, "seq", split_axis=0, concat_axis=0, tiled=True)
    patches = (
        patches.reshape(seq_count, patch_rows, patch_cols, 4 * channels)
        .transpose(1, 0, 2, 3)
        .reshape(full, 4 * channels)
    )
    stream_grad = jnp.dot(patches, final_weight, preferred_element_type=jnp.float32)
    gate_row = lax.dynamic_slice_in_dim(gate_table, bucket[0], 1, 0).astype(jnp.float32)
    branch_grad = (stream_grad * gate_row).astype(jnp.bfloat16)
    group_weight = lax.dynamic_slice_in_dim(out_weight, seq_index * group, group, 0)
    attn_grad = lax.dot_general(
        branch_grad, group_weight, (((1,), (1,)), ((), ())), preferred_element_type=jnp.float32
    ).astype(jnp.bfloat16)

    qk_grad, v_grad = attention_backward(qkv, attn_grad)
    v_grad = lax.all_to_all(v_grad, "seq", split_axis=0, concat_axis=0, tiled=True)
    value_grad = v_grad.transpose(1, 0, 2).reshape(tokens, width)
    values = lax.all_gather(value_grad, "dp", axis=0, tiled=True)
    qk_grad = lax.all_to_all(qk_grad, "seq", split_axis=0, concat_axis=0, tiled=True)
    qk_grad = qk_grad.transpose(1, 2, 0, 3).reshape(2, tokens, width)
    term = lax.dot_general(
        inputs, values, (((0,), (0,)), ((), ())), preferred_element_type=jnp.float32
    ).astype(jnp.bfloat16)
    terms = lax.all_to_all(
        term.reshape(seq_count, rows_block // seq_count, width),
        "seq", split_axis=0, concat_axis=0, tiled=True,
    )
    weight_grad = jnp.sum(terms.astype(jnp.float32), axis=0)
    return (qk_grad[:1], qk_grad[1:], value_grad[None], weight_grad)


def solution(mesh):
    return jax.shard_map(
        per_device,
        mesh=mesh,
        in_specs=(
            P("dp", None, "seq", None),
            P("dp", None, "seq", None),
            P(),
            P(),
            P(),
            P(),
            P("dp"),
            P("dp", "seq", None),
            P("dp", "seq", None),
            P("dp", "seq", None),
            P(),
            P("dp", "seq", None),
        ),
        out_specs=(
            P("dp", "seq", None),
            P("dp", "seq", None),
            P("dp", "seq", None),
            P(("dp", "seq"), None),
        ),
        check_vma=False,
    )
```

```python
import functools

import jax
import jax.numpy as jnp
from jax import lax
from jax.experimental import pallas as pl
from jax.experimental.pallas import tpu as pltpu
from jax.sharding import PartitionSpec as P

DH = 128


def silu_slope(values):
    sigma = jax.nn.sigmoid(values)
    return sigma * (1.0 + values * (1.0 - sigma))


def conv_grad(grad, kernel, rows_pad):
    flipped = jnp.transpose(kernel[::-1, ::-1], (0, 1, 3, 2))
    return lax.conv_general_dilated(
        grad,
        flipped,
        (1, 1),
        (rows_pad, (0, 0)),
        dimension_numbers=("NHWC", "HWIO", "NHWC"),
        preferred_element_type=jnp.float32,
    )


def head_kernel(q_ref, k_ref, v_ref, g_ref, qk_out, v_out):
    softmax_scale = DH ** (-0.5)
    blocks, _, rows, _ = q_ref.shape
    full = blocks * rows
    q_head = q_ref[:, 0].reshape(full, DH)
    k_head = k_ref[:, 0].reshape(full, DH)
    v_head = v_ref[:, 0].reshape(full, DH)
    g_head = g_ref[...]

    def rows_by_rows(a, b):
        return lax.dot_general(a, b, (((1,), (1,)), ((), ())), preferred_element_type=jnp.float32)

    def columns_by_columns(a, b):
        return lax.dot_general(a, b, (((0,), (0,)), ((), ())), preferred_element_type=jnp.float32)

    scores = rows_by_rows(q_head, k_head) * softmax_scale
    weights = jnp.exp(scores - jnp.max(scores, axis=1, keepdims=True))
    probs = weights * (1.0 / jnp.sum(weights, axis=1, keepdims=True))
    probs_low = probs.astype(jnp.bfloat16)
    head_out = jnp.dot(probs_low, v_head, preferred_element_type=jnp.float32).astype(jnp.bfloat16)
    row_dot = jnp.sum(
        g_head.astype(jnp.float32) * head_out.astype(jnp.float32), axis=1, keepdims=True
    )
    prob_grad = rows_by_rows(g_head, v_head)
    score_grad = (probs * (prob_grad - row_dot)).astype(jnp.bfloat16)
    q_grad = jnp.dot(score_grad, k_head, preferred_element_type=jnp.float32) * softmax_scale
    k_grad = columns_by_columns(score_grad, q_head) * softmax_scale
    v_grad = columns_by_columns(probs_low, g_head)
    qk_out[:, 0] = q_grad.astype(jnp.bfloat16).reshape(blocks, rows, DH)
    qk_out[:, 1] = k_grad.astype(jnp.bfloat16).reshape(blocks, rows, DH)
    v_out[...] = v_grad.astype(jnp.bfloat16).reshape(blocks, rows, DH)


def attention_backward(qkv, grad):
    blocks, _, rows, group = qkv.shape
    full = blocks * rows

    def part(which):
        return pl.BlockSpec((blocks, 1, rows, DH), lambda h: (0, which, 0, h))

    heads = group // DH
    return pl.pallas_call(
        head_kernel,
        grid=(heads,),
        in_specs=[part(0), part(1), part(2), pl.BlockSpec((full, DH), lambda h: (0, h))],
        out_specs=[
            pl.BlockSpec((blocks, 2, rows, DH), lambda h: (0, 0, 0, h)),
            pl.BlockSpec((blocks, rows, DH), lambda h: (0, 0, h)),
        ],
        out_shape=[
            jax.ShapeDtypeStruct((blocks, 2, rows, group), jnp.bfloat16),
            jax.ShapeDtypeStruct((blocks, rows, group), jnp.bfloat16),
        ],
        compiler_params=pltpu.CompilerParams(vmem_limit_bytes=48 * 2**20),
        cost_estimate=pl.CostEstimate(
            flops=14 * heads * full * full * DH,
            bytes_accessed=14 * full * group,
            transcendentals=heads * full * full,
        ),
    )(qkv, qkv, qkv, grad)


def return_kernel(seq_count, dp_count, v_ref, qk_ref, x_ref, qk_out, v_out, w_out,
                  own, gathered, terms, arrived, x_send, x_recv, v_send, v_recv,
                  qk_send, qk_recv, g_send, g_recv, t_send, t_recv, here):
    seq_index, dp_index = lax.axis_index("seq"), lax.axis_index("dp")
    _, tokens, group = v_ref.shape

    def seq_peer(step):
        return lax.rem(seq_index + step, seq_count)

    def dp_peer(step):
        return lax.rem(dp_index + step, dp_count)

    def columns(block):
        return pl.ds(pl.multiple_of(block * group, group), group)

    def slot(step):
        return pl.ds(step * tokens, tokens)

    def to_seq(source, target, send, recv, step):
        return pltpu.make_async_remote_copy(
            src_ref=source, dst_ref=target, send_sem=send, recv_sem=recv,
            device_id={"seq": seq_peer(step)}, device_id_type=pl.DeviceIdType.MESH,
        )

    def to_dp(source, target, send, recv, step):
        return pltpu.make_async_remote_copy(
            src_ref=source, dst_ref=target, send_sem=send, recv_sem=recv,
            device_id={"dp": dp_peer(step)}, device_id_type=pl.DeviceIdType.MESH,
        )

    barrier = pltpu.get_barrier_semaphore()
    for step in range(1, seq_count):
        pl.semaphore_signal(
            barrier, inc=1, device_id={"seq": seq_peer(step)}, device_id_type=pl.DeviceIdType.MESH
        )
    for step in range(1, dp_count):
        pl.semaphore_signal(
            barrier, inc=1, device_id={"dp": dp_peer(step)}, device_id_type=pl.DeviceIdType.MESH
        )
    pl.semaphore_wait(barrier, seq_count + dp_count - 2)

    v_copies = [
        to_seq(v_ref.at[seq_peer(e)], gathered.at[e, slot(0)], v_send.at[e], v_recv.at[e], e)
        for e in range(1, seq_count)
    ]
    for copy in v_copies:
        copy.start()
    x_copies = [
        to_dp(x_ref.at[dp_peer(d)], own.at[slot(d)], x_send.at[d], x_recv.at[d], d)
        for d in range(1, dp_count)
    ]
    for copy in x_copies:
        copy.start()
    gathered[0, slot(0)] = v_ref[seq_index]

    def gather(c):
        copies = [
            to_dp(
                gathered.at[c, slot(0)], gathered.at[c, slot(d)], g_send.at[c, d], g_recv.at[c, d], d
            )
            for d in range(1, dp_count)
        ]
        for copy in copies:
            copy.start()
        return copies

    g_copies = [gather(0)]
    qk_copies = [
        to_seq(
            qk_ref.at[seq_peer(e)], qk_out.at[:, :, columns(seq_index)],
            qk_send.at[e], qk_recv.at[e], e,
        )
        for e in range(1, seq_count)
    ]
    for copy in qk_copies:
        copy.start()
    mine = pltpu.make_async_copy(
        qk_ref.at[seq_index], qk_out.at[:, :, columns(seq_index)], here.at[0]
    )
    mine.start()
    own[slot(0)] = x_ref[dp_index]
    for c in range(1, seq_count):
        v_copies[c - 1].wait_recv()
        g_copies.append(gather(c))
    for c in range(seq_count):
        v_out[:, columns(lax.rem(seq_index + seq_count - c, seq_count))] = gathered[c, slot(0)]
    for copy in x_copies:
        copy.wait_recv()

    t_copies = []
    for c in range(seq_count):
        for copy in g_copies[c]:
            copy.wait_recv()
        term = lax.dot_general(
            own[...], gathered[c], (((0,), (0,)), ((), ())), preferred_element_type=jnp.float32
        )
        rows = term.shape[0] // seq_count
        for j in range(seq_count):
            terms[c, j] = term[j * rows : (j + 1) * rows].astype(jnp.bfloat16)
        sends = [
            to_seq(
                terms.at[c, seq_peer(e)], arrived.at[e, c], t_send.at[e, c], t_recv.at[e, c], e
            )
            for e in range(1, seq_count)
        ]
        for copy in sends:
            copy.start()
        t_copies.append(sends)

    for k in range(seq_count):
        total = terms[k, seq_index].astype(jnp.float32)
        for e in range(1, seq_count):
            c = (k - e) % seq_count
            t_copies[c][e - 1].wait_recv()
            total += arrived[e, c].astype(jnp.float32)
        w_out[:, columns(lax.rem(seq_index + seq_count - k, seq_count))] = total
    mine.wait()
    for copy in qk_copies:
        copy.wait_recv()
    for copy in v_copies + x_copies + qk_copies:
        copy.wait_send()
    for copies in g_copies + t_copies:
        for copy in copies:
            copy.wait_send()


def return_grads(v_grad, qk_grad, inputs):
    seq_count, tokens, group = v_grad.shape
    dp_count, _, rows_block = inputs.shape
    width = seq_count * group
    rows = rows_block // seq_count
    vmem = pl.BlockSpec(memory_space=pltpu.VMEM)

    def pair(*shape):
        return [pltpu.SemaphoreType.DMA(shape), pltpu.SemaphoreType.DMA(shape)]

    return pl.pallas_call(
        functools.partial(return_kernel, seq_count, dp_count),
        in_specs=[vmem] * 3,
        out_specs=[vmem] * 3,
        out_shape=[
            jax.ShapeDtypeStruct((2, tokens, width), jnp.bfloat16),
            jax.ShapeDtypeStruct((tokens, width), jnp.bfloat16),
            jax.ShapeDtypeStruct((rows, width), jnp.float32),
        ],
        scratch_shapes=[
            pltpu.VMEM((dp_count * tokens, rows_block), jnp.bfloat16),
            pltpu.VMEM((seq_count, dp_count * tokens, group), jnp.bfloat16),
            pltpu.VMEM((seq_count, seq_count, rows, group), jnp.bfloat16),
            pltpu.VMEM((seq_count, seq_count, rows, group), jnp.bfloat16),
        ]
        + pair(dp_count)
        + pair(seq_count)
        + pair(seq_count)
        + pair(seq_count, dp_count)
        + pair(seq_count, seq_count)
        + [pltpu.SemaphoreType.DMA((1,))],
        compiler_params=pltpu.CompilerParams(
            collective_id=0, has_side_effects=True, vmem_limit_bytes=40 * 2**20
        ),
        cost_estimate=pl.CostEstimate(
            flops=2 * dp_count * tokens * rows_block * width,
            bytes_accessed=8 * tokens * width * dp_count,
            transcendentals=0,
        ),
    )(v_grad, qk_grad, inputs)


def per_device(
    pre_activation,
    output_grad,
    up_kernel,
    in_kernel,
    final_weight,
    gate_table,
    bucket,
    query_vectors,
    key_vectors,
    value_vectors,
    out_weight,
    block_input,
):
    seq_count = lax.axis_size("seq")
    dp_count = lax.axis_size("dp")
    seq_index = lax.axis_index("seq")
    tokens, width = query_vectors.shape[1:]
    group = width // seq_count
    full = tokens * seq_count
    model = block_input.shape[2]

    forward = [(i, i + 1) for i in range(seq_count - 1)]
    backward = [(target, source) for source, target in forward]
    low = lax.ppermute(
        jnp.concatenate([output_grad[:, :, -2:], pre_activation[:, :, -1:]], axis=2), "seq", forward
    )
    high = lax.ppermute(
        jnp.concatenate([output_grad[:, :, :2], pre_activation[:, :, :1]], axis=2), "seq", backward
    )
    qkv = jnp.stack([query_vectors[0], key_vectors[0], value_vectors[0]])
    qkv = qkv.reshape(3, tokens, seq_count, group).transpose(2, 0, 1, 3)
    qkv = lax.all_to_all(qkv, "seq", split_axis=0, concat_axis=0, tiled=True)
    rows_block = model // dp_count
    inputs = block_input[0].reshape(tokens, dp_count, rows_block).transpose(1, 0, 2)

    wide_grad = jnp.concatenate([low[:, :, :2], output_grad, high[:, :, :2]], axis=2)
    wide_pre = jnp.concatenate([low[:, :, 2:], pre_activation, high[:, :, 2:]], axis=2)
    act_grad = conv_grad(wide_grad, up_kernel, (1, 1))
    columns = jnp.arange(wide_pre.shape[2])
    inside = ((columns > 0) | (seq_index > 0)) & (
        (columns < wide_pre.shape[2] - 1) | (seq_index < seq_count - 1)
    )
    feat_grad = act_grad * silu_slope(wide_pre.astype(jnp.float32))
    feat_grad = jnp.where(inside[None, None, :, None], feat_grad, 0.0).astype(jnp.bfloat16)
    latent_grad = conv_grad(feat_grad, in_kernel, (1, 1)).astype(jnp.bfloat16)

    _, lat_rows, lat_cols, channels = latent_grad.shape
    patch_rows, patch_cols = lat_rows // 2, lat_cols // 2
    patches = (
        latent_grad.reshape(patch_rows, 2, patch_cols, 2, channels)
        .transpose(0, 2, 1, 3, 4)
        .reshape(1, patch_rows * patch_cols, 4 * channels)
    )
    qkv, patches = lax.optimization_barrier((qkv, patches))
    patches = jnp.broadcast_to(patches, (seq_count,) + patches.shape[1:])
    patches = lax.all_to_all(patches, "seq", split_axis=0, concat_axis=0, tiled=True)
    patches = (
        patches.reshape(seq_count, patch_rows, patch_cols, 4 * channels)
        .transpose(1, 0, 2, 3)
        .reshape(full, 4 * channels)
    )
    stream_grad = jnp.dot(patches, final_weight, preferred_element_type=jnp.float32)
    gate_row = lax.dynamic_slice_in_dim(gate_table, bucket[0], 1, 0).astype(jnp.float32)
    branch_grad = (stream_grad * gate_row).astype(jnp.bfloat16)
    group_weight = lax.dynamic_slice_in_dim(out_weight, seq_index * group, group, 0)
    attn_grad = lax.dot_general(
        branch_grad, group_weight, (((1,), (1,)), ((), ())), preferred_element_type=jnp.float32
    ).astype(jnp.bfloat16)

    qk_grad, v_grad = attention_backward(qkv, attn_grad)
    qk_grad, value_grad, weight_grad = return_grads(v_grad, qk_grad, inputs)
    return (qk_grad[:1], qk_grad[1:], value_grad[None], weight_grad)


def solution(mesh):
    return jax.shard_map(
        per_device,
        mesh=mesh,
        in_specs=(
            P("dp", None, "seq", None),
            P("dp", None, "seq", None),
            P(),
            P(),
            P(),
            P(),
            P("dp"),
            P("dp", "seq", None),
            P("dp", "seq", None),
            P("dp", "seq", None),
            P(),
            P("dp", "seq", None),
        ),
        out_specs=(
            P("dp", "seq", None),
            P("dp", "seq", None),
            P("dp", "seq", None),
            P(("dp", "seq"), None),
        ),
        check_vma=False,
    )
```

```python
import functools

import jax
import jax.numpy as jnp
from jax import lax
from jax.experimental import pallas as pl
from jax.experimental.pallas import tpu as pltpu
from jax.sharding import PartitionSpec as P

DH = 128


def silu_slope(values):
    sigma = jax.nn.sigmoid(values)
    return sigma * (1.0 + values * (1.0 - sigma))


def conv_grad(grad, kernel, rows_pad):
    flipped = jnp.transpose(kernel[::-1, ::-1], (0, 1, 3, 2))
    return lax.conv_general_dilated(
        grad,
        flipped,
        (1, 1),
        (rows_pad, (0, 0)),
        dimension_numbers=("NHWC", "HWIO", "NHWC"),
        preferred_element_type=jnp.float32,
    )


def head_kernel(q_ref, k_ref, v_ref, g_ref, qk_out, v_out):
    softmax_scale = DH ** (-0.5)
    blocks, _, rows, _ = q_ref.shape
    full = blocks * rows
    q_head = q_ref[:, 0].reshape(full, DH)
    k_head = k_ref[:, 0].reshape(full, DH)
    v_head = v_ref[:, 0].reshape(full, DH)
    g_head = g_ref[...]

    def rows_by_rows(a, b):
        return lax.dot_general(a, b, (((1,), (1,)), ((), ())), preferred_element_type=jnp.float32)

    def columns_by_columns(a, b):
        return lax.dot_general(a, b, (((0,), (0,)), ((), ())), preferred_element_type=jnp.float32)

    scores = rows_by_rows(q_head, k_head) * softmax_scale
    weights = jnp.exp(scores - jnp.max(scores, axis=1, keepdims=True))
    probs = weights * (1.0 / jnp.sum(weights, axis=1, keepdims=True))
    probs_low = probs.astype(jnp.bfloat16)
    head_out = jnp.dot(probs_low, v_head, preferred_element_type=jnp.float32).astype(jnp.bfloat16)
    row_dot = jnp.sum(
        g_head.astype(jnp.float32) * head_out.astype(jnp.float32), axis=1, keepdims=True
    )
    prob_grad = rows_by_rows(g_head, v_head)
    score_grad = (probs * (prob_grad - row_dot)).astype(jnp.bfloat16)
    q_grad = jnp.dot(score_grad, k_head, preferred_element_type=jnp.float32) * softmax_scale
    k_grad = columns_by_columns(score_grad, q_head) * softmax_scale
    v_grad = columns_by_columns(probs_low, g_head)
    qk_out[:, 0] = q_grad.astype(jnp.bfloat16).reshape(blocks, rows, DH)
    qk_out[:, 1] = k_grad.astype(jnp.bfloat16).reshape(blocks, rows, DH)
    v_out[...] = v_grad.astype(jnp.bfloat16).reshape(blocks, rows, DH)


def attention_backward(qkv, grad):
    blocks, _, rows, group = qkv.shape
    full = blocks * rows

    def part(which):
        return pl.BlockSpec((blocks, 1, rows, DH), lambda h: (0, which, 0, h))

    heads = group // DH
    return pl.pallas_call(
        head_kernel,
        grid=(heads,),
        in_specs=[part(0), part(1), part(2), pl.BlockSpec((full, DH), lambda h: (0, h))],
        out_specs=[
            pl.BlockSpec((blocks, 2, rows, DH), lambda h: (0, 0, 0, h)),
            pl.BlockSpec((blocks, rows, DH), lambda h: (0, 0, h)),
        ],
        out_shape=[
            jax.ShapeDtypeStruct((blocks, 2, rows, group), jnp.bfloat16),
            jax.ShapeDtypeStruct((blocks, rows, group), jnp.bfloat16),
        ],
        compiler_params=pltpu.CompilerParams(vmem_limit_bytes=48 * 2**20),
        cost_estimate=pl.CostEstimate(
            flops=14 * heads * full * full * DH,
            bytes_accessed=14 * full * group,
            transcendentals=heads * full * full,
        ),
    )(qkv, qkv, qkv, grad)


def return_kernel(seq_count, dp_count, v_ref, qk_ref, x_ref, qk_out, v_out, w_out,
                  own, gathered, terms, arrived, x_send, x_recv, v_send, v_recv,
                  qk_send, qk_recv, g_send, g_recv, t_send, t_recv, here):
    seq_index, dp_index = lax.axis_index("seq"), lax.axis_index("dp")
    _, tokens, group = v_ref.shape

    def seq_peer(step):
        return lax.rem(seq_index + step, seq_count)

    def dp_peer(step):
        return lax.rem(dp_index + step, dp_count)

    def columns(block):
        return pl.ds(pl.multiple_of(block * group, group), group)

    def slot(step):
        return pl.ds(step * tokens, tokens)

    def to_seq(source, target, send, recv, step):
        return pltpu.make_async_remote_copy(
            src_ref=source, dst_ref=target, send_sem=send, recv_sem=recv,
            device_id={"seq": seq_peer(step)}, device_id_type=pl.DeviceIdType.MESH,
        )

    def to_dp(source, target, send, recv, step):
        return pltpu.make_async_remote_copy(
            src_ref=source, dst_ref=target, send_sem=send, recv_sem=recv,
            device_id={"dp": dp_peer(step)}, device_id_type=pl.DeviceIdType.MESH,
        )

    barrier = pltpu.get_barrier_semaphore()
    for step in range(1, seq_count):
        pl.semaphore_signal(
            barrier, inc=1, device_id={"seq": seq_peer(step)}, device_id_type=pl.DeviceIdType.MESH
        )
    for step in range(1, dp_count):
        pl.semaphore_signal(
            barrier, inc=1, device_id={"dp": dp_peer(step)}, device_id_type=pl.DeviceIdType.MESH
        )
    pl.semaphore_wait(barrier, seq_count + dp_count - 2)

    v_copies = [
        to_seq(v_ref.at[seq_peer(e)], gathered.at[e, slot(0)], v_send.at[e], v_recv.at[e], e)
        for e in range(1, seq_count)
    ]
    for copy in v_copies:
        copy.start()
    x_copies = [
        to_dp(x_ref.at[dp_peer(d)], own.at[slot(d)], x_send.at[d], x_recv.at[d], d)
        for d in range(1, dp_count)
    ]
    for copy in x_copies:
        copy.start()
    gathered[0, slot(0)] = v_ref[seq_index]

    def gather(c):
        copies = [
            to_dp(
                gathered.at[c, slot(0)], gathered.at[c, slot(d)], g_send.at[c, d], g_recv.at[c, d], d
            )
            for d in range(1, dp_count)
        ]
        for copy in copies:
            copy.start()
        return copies

    g_copies = [gather(0)]
    qk_copies = [
        to_seq(
            qk_ref.at[seq_peer(e)], qk_out.at[:, :, columns(seq_index)],
            qk_send.at[e], qk_recv.at[e], e,
        )
        for e in range(1, seq_count)
    ]
    for copy in qk_copies:
        copy.start()
    mine = pltpu.make_async_copy(
        qk_ref.at[seq_index], qk_out.at[:, :, columns(seq_index)], here.at[0]
    )
    mine.start()
    own[slot(0)] = x_ref[dp_index]
    for c in range(1, seq_count):
        v_copies[c - 1].wait_recv()
        g_copies.append(gather(c))
    for c in range(seq_count):
        v_out[:, columns(lax.rem(seq_index + seq_count - c, seq_count))] = gathered[c, slot(0)]
    for copy in x_copies:
        copy.wait_recv()

    t_copies = []
    for c in range(seq_count):
        for copy in g_copies[c]:
            copy.wait_recv()
        term = lax.dot_general(
            own[...], gathered[c], (((0,), (0,)), ((), ())), preferred_element_type=jnp.float32
        )
        rows = term.shape[0] // seq_count
        for j in range(seq_count):
            terms[c, j] = term[j * rows : (j + 1) * rows].astype(jnp.bfloat16)
        sends = [
            to_seq(
                terms.at[c, seq_peer(e)], arrived.at[e, c], t_send.at[e, c], t_recv.at[e, c], e
            )
            for e in range(1, seq_count)
        ]
        for copy in sends:
            copy.start()
        t_copies.append(sends)

    for k in range(seq_count):
        total = terms[k, seq_index].astype(jnp.float32)
        for e in range(1, seq_count):
            c = (k - e) % seq_count
            t_copies[c][e - 1].wait_recv()
            total += arrived[e, c].astype(jnp.float32)
        w_out[:, columns(lax.rem(seq_index + seq_count - k, seq_count))] = total
    mine.wait()
    for copy in qk_copies:
        copy.wait_recv()
    for copy in v_copies + x_copies + qk_copies:
        copy.wait_send()
    for copies in g_copies + t_copies:
        for copy in copies:
            copy.wait_send()


def return_grads(v_grad, qk_grad, inputs):
    seq_count, tokens, group = v_grad.shape
    dp_count, _, rows_block = inputs.shape
    width = seq_count * group
    rows = rows_block // seq_count
    vmem = pl.BlockSpec(memory_space=pltpu.VMEM)

    def pair(*shape):
        return [pltpu.SemaphoreType.DMA(shape), pltpu.SemaphoreType.DMA(shape)]

    return pl.pallas_call(
        functools.partial(return_kernel, seq_count, dp_count),
        in_specs=[vmem] * 3,
        out_specs=[vmem] * 3,
        out_shape=[
            jax.ShapeDtypeStruct((2, tokens, width), jnp.bfloat16),
            jax.ShapeDtypeStruct((tokens, width), jnp.bfloat16),
            jax.ShapeDtypeStruct((rows, width), jnp.float32),
        ],
        scratch_shapes=[
            pltpu.VMEM((dp_count * tokens, rows_block), jnp.bfloat16),
            pltpu.VMEM((seq_count, dp_count * tokens, group), jnp.bfloat16),
            pltpu.VMEM((seq_count, seq_count, rows, group), jnp.bfloat16),
            pltpu.VMEM((seq_count, seq_count, rows, group), jnp.bfloat16),
        ]
        + pair(dp_count)
        + pair(seq_count)
        + pair(seq_count)
        + pair(seq_count, dp_count)
        + pair(seq_count, seq_count)
        + [pltpu.SemaphoreType.DMA((1,))],
        compiler_params=pltpu.CompilerParams(
            collective_id=0, has_side_effects=True, vmem_limit_bytes=40 * 2**20
        ),
        cost_estimate=pl.CostEstimate(
            flops=2 * dp_count * tokens * rows_block * width,
            bytes_accessed=8 * tokens * width * dp_count,
            transcendentals=0,
        ),
    )(v_grad, qk_grad, inputs)


def per_device(
    pre_activation,
    output_grad,
    up_kernel,
    in_kernel,
    final_weight,
    gate_table,
    bucket,
    query_vectors,
    key_vectors,
    value_vectors,
    out_weight,
    block_input,
):
    seq_count = lax.axis_size("seq")
    dp_count = lax.axis_size("dp")
    seq_index = lax.axis_index("seq")
    tokens, width = query_vectors.shape[1:]
    group = width // seq_count
    full = tokens * seq_count
    model = block_input.shape[2]

    forward = [(i, i + 1) for i in range(seq_count - 1)]
    backward = [(target, source) for source, target in forward]
    low = lax.ppermute(
        jnp.concatenate([output_grad[:, :, -2:], pre_activation[:, :, -1:]], axis=2), "seq", forward
    )
    high = lax.ppermute(
        jnp.concatenate([output_grad[:, :, :2], pre_activation[:, :, :1]], axis=2), "seq", backward
    )
    qkv = jnp.stack([query_vectors[0], key_vectors[0], value_vectors[0]])
    qkv = qkv.reshape(3, tokens, seq_count, group).transpose(2, 0, 1, 3)
    qkv = lax.all_to_all(qkv, "seq", split_axis=0, concat_axis=0, tiled=True)
    rows_block = model // dp_count
    inputs = block_input[0].reshape(tokens, dp_count, rows_block).transpose(1, 0, 2)

    wide_grad = jnp.concatenate([low[:, :, :2], output_grad, high[:, :, :2]], axis=2)
    wide_pre = jnp.concatenate([low[:, :, 2:], pre_activation, high[:, :, 2:]], axis=2)
    act_grad = conv_grad(wide_grad, up_kernel, (1, 1))
    act_grad = lax.optimization_barrier(act_grad)
    columns = jnp.arange(wide_pre.shape[2])
    inside = ((columns > 0) | (seq_index > 0)) & (
        (columns < wide_pre.shape[2] - 1) | (seq_index < seq_count - 1)
    )
    feat_grad = act_grad * silu_slope(wide_pre.astype(jnp.float32))
    feat_grad = jnp.where(inside[None, None, :, None], feat_grad, 0.0).astype(jnp.bfloat16)
    latent_grad = conv_grad(feat_grad, in_kernel, (1, 1)).astype(jnp.bfloat16)

    _, lat_rows, lat_cols, channels = latent_grad.shape
    patch_rows, patch_cols = lat_rows // 2, lat_cols // 2
    patches = (
        latent_grad.reshape(patch_rows, 2, patch_cols, 2, channels)
        .transpose(0, 2, 1, 3, 4)
        .reshape(1, patch_rows * patch_cols, 4 * channels)
    )
    qkv, patches = lax.optimization_barrier((qkv, patches))
    patches = jnp.broadcast_to(patches, (seq_count,) + patches.shape[1:])
    patches = lax.all_to_all(patches, "seq", split_axis=0, concat_axis=0, tiled=True)
    patches = (
        patches.reshape(seq_count, patch_rows, patch_cols, 4 * channels)
        .transpose(1, 0, 2, 3)
        .reshape(full, 4 * channels)
    )
    stream_grad = jnp.dot(patches, final_weight, preferred_element_type=jnp.float32)
    gate_row = lax.dynamic_slice_in_dim(gate_table, bucket[0], 1, 0).astype(jnp.float32)
    branch_grad = (stream_grad * gate_row).astype(jnp.bfloat16)
    group_weight = lax.dynamic_slice_in_dim(out_weight, seq_index * group, group, 0)
    attn_grad = lax.dot_general(
        branch_grad, group_weight, (((1,), (1,)), ((), ())), preferred_element_type=jnp.float32
    ).astype(jnp.bfloat16)

    qk_grad, v_grad = attention_backward(qkv, attn_grad)
    qk_grad, value_grad, weight_grad = return_grads(v_grad, qk_grad, inputs)
    return (qk_grad[:1], qk_grad[1:], value_grad[None], weight_grad)


def solution(mesh):
    return jax.shard_map(
        per_device,
        mesh=mesh,
        in_specs=(
            P("dp", None, "seq", None),
            P("dp", None, "seq", None),
            P(),
            P(),
            P(),
            P(),
            P("dp"),
            P("dp", "seq", None),
            P("dp", "seq", None),
            P("dp", "seq", None),
            P(),
            P("dp", "seq", None),
        ),
        out_specs=(
            P("dp", "seq", None),
            P("dp", "seq", None),
            P("dp", "seq", None),
            P(("dp", "seq"), None),
        ),
        check_vma=False,
    )
```
